32 devices in a mesh: section: 2 (over x), expert: 8 (over z, core), dp: 2 (over y).
Axes of the slice: x: 2, y: 2, z: 4, core: 2. Of those that a mesh axis runs over, the one named last changes fastest.
Arguments:
- fwd_input: bfloat16 [2, 768, 3584], P('section', ('expert', 'dp')), may hold values from -24 to 24
- back_saved: bfloat16 [2, 2, 768, 3584], P(None, 'section', ('expert', 'dp')), may hold values from -24 to 24
- back_grad: bfloat16 [2, 768, 3584], P('section', ('expert', 'dp')), may hold values from -6 to 6
- norm_gain: float32 [2, 3584], P('section'), may hold values from 0.3 to 3
- gate_weight: bfloat16 [2, 8, 3584, 1024], P('section', 'expert', 'dp'), may hold values from -0.09375 to 0.09375
- up_weight: bfloat16 [2, 8, 3584, 1024], P('section', 'expert', 'dp'), may hold values from -0.09375 to 0.09375
- down_weight: bfloat16 [2, 8, 1024, 3584], P('section', 'expert', None, 'dp'), may hold values from -0.1875 to 0.1875
- routes: int32 [4, 2, 768, 2], P(None, 'section', ('expert', 'dp')), may hold values from 0 to 7, as said below
- slots: int32 [4, 2, 768, 2], P(None, 'section', ('expert', 'dp')), may hold values from 0 to 12, as said below
- affinity: float32 [4, 2, 768, 2], P(None, 'section', ('expert', 'dp')), may hold values from 0.05 to 1
Outputs:
- fwd_output: bfloat16 [2, 768, 3584], P('section', ('expert', 'dp'))
- back_output: bfloat16 [2, 768, 3584], P('section', ('expert', 'dp'))
The draws below stay inside these ranges and needn't reach their ends.
Inputs may be any that keep to these rules, and one draw needn't show every extreme that they name: A token's routes name distinct experts. In each aligned block of 48 tokens of one index of the first dimension and one section, each expert is named at most 13 times, and one expert exactly 13 times; that expert is the same for all blocks of one index of the first dimension, one section and one dp index. Within one aligned block of 48 tokens, the routes to one expert hold distinct slots.
All inputs are finite; a program needn't handle non-finite values.
Results may differ from the reference program's by a relative error of at most 0.012.
Values may be sent and summed in bfloat16 or wider, within the bound.
A program may use at most 128 MiB of HBM per device.

```python
import math
import jax
import jax.numpy as jnp
from jax import lax

D = 3584
H = 1024
TOPK = 2
TOK_DEV = 48
EXPERTS = 8
TOKENS = 768
CAP = 13
N_SECTION = 2
N_EXPERT = 8
N_DP = 2


def route_cells(key):
    blocks = 4 * N_SECTION * N_EXPERT * N_DP
    cells = EXPERTS * CAP
    chosen_count = TOK_DEV * TOPK
    key_full, key_rank, key_order, key_turn = jax.random.split(key, 4)
    full = jax.random.randint(key_full, (4, N_SECTION, 1, N_DP), 0, EXPERTS)
    full = jnp.broadcast_to(full, (4, N_SECTION, N_EXPERT, N_DP)).reshape(blocks, 1)
    cell_ids = jnp.arange(cells, dtype=jnp.int32)[None, :]
    ranking = jax.random.randint(key_rank, (blocks, cells), 0, 1 << 20) * cells + cell_ids
    ranking = jnp.where(cell_ids // CAP == full, -1, ranking)
    picked = jnp.argsort(ranking, axis=1, stable=True)[:, :chosen_count].astype(jnp.int32)
    picked = jnp.sort(picked, axis=1)
    layout = jnp.transpose(picked.reshape(blocks, TOPK, TOK_DEV), (0, 2, 1))
    token_ids = jnp.arange(TOK_DEV, dtype=jnp.int32)[None, :]
    order = jnp.argsort(jax.random.randint(key_order, (blocks, TOK_DEV), 0, 1 << 20) * TOK_DEV + token_ids, axis=1)
    layout = jnp.take_along_axis(layout, order[:, :, None].astype(jnp.int32), axis=1)
    turn = jax.random.randint(key_turn, (blocks, TOK_DEV, 1), 0, TOPK)
    columns = (jnp.arange(TOPK, dtype=jnp.int32)[None, None, :] + turn) % TOPK
    layout = jnp.take_along_axis(layout, columns, axis=2)
    return layout.reshape(4, N_SECTION, N_EXPERT * N_DP * TOK_DEV, TOPK)


def draw_routes(key, part):
    return (route_cells(key) // CAP).astype(jnp.int32)


def draw_slots(key, part):
    return (route_cells(key) % CAP).astype(jnp.int32)


def feature_field(key, shape):
    key_normal = jax.random.fold_in(key, 0)
    key_rows = jax.random.fold_in(key, 2)
    key_cols = jax.random.fold_in(key, 3)
    base = jax.random.normal(key_normal, shape, jnp.float32)
    row_scale = jnp.exp(jax.random.uniform(key_rows, shape[:-1] + (1,), jnp.float32, minval=math.log(0.3), maxval=math.log(3.0)))
    col_scale = jnp.exp(jax.random.uniform(key_cols, (shape[-1],), jnp.float32, minval=math.log(0.3), maxval=math.log(3.0)))
    return jnp.clip(base * row_scale * col_scale, -24.0, 24.0)


def draw_fwd_input(key, part):
    key = jax.random.fold_in(key, 1)
    field = feature_field(key, (N_SECTION, TOKENS, D))
    return field.astype(jnp.bfloat16)


def draw_back_saved(key, part):
    key = jax.random.fold_in(key, 2)
    field = feature_field(key, (2, N_SECTION, TOKENS, D))
    return field.astype(jnp.bfloat16)


def levels(own_key, extent, cuts, least, top_value):
    def one(dim, blocks):
        steps = jax.random.uniform(jax.random.fold_in(jax.random.fold_in(own_key, 6), dim), (blocks,), jnp.float32, least / len(cuts), top_value / len(cuts))
        return jnp.repeat(jnp.exp(steps), extent[dim] // blocks).reshape((-1,) + (1,) * (len(extent) - dim - 1))

    factor_of = one(*cuts[0])
    for cut in cuts[1:]:
        factor_of = factor_of * one(*cut)
    return factor_of


def bell_draw(own_key, shape, scale, most, cuts=(), held_as=jnp.bfloat16):
    level = levels(own_key, shape, cuts, -0.22, 0.18) if cuts else 1.0
    drawn = jax.random.normal(own_key, shape, jnp.float32) * scale * level
    return jnp.minimum(jnp.maximum(drawn, -most), most).astype(held_as)


def setup_inputs(seed: int = 0) -> dict:
    seeds = jax.random.split(jax.random.key(seed), 11)
    fwd_input = draw_fwd_input(jax.random.fold_in(seeds[10], 71), 0)
    back_saved = draw_back_saved(jax.random.fold_in(seeds[10], 71), 0)
    back_grad = bell_draw(seeds[2], (N_SECTION, TOKENS, D), 1.0, 6.0, ((0, 2), (1, 16)))
    norm_gain = jnp.clip(jnp.exp(math.log(3.0) - 2.3025851 * jax.random.uniform(seeds[3], (N_SECTION, D), jnp.float32) ** levels(seeds[3], (N_SECTION, D), ((0, 2),), -0.2, 0.2)), 0.3, 3.0)
    gate_weight = bell_draw(seeds[4], (N_SECTION, EXPERTS, D, H), D ** -0.5, 0.09375, ((0, 2), (1, 8), (2, 2)))
    up_weight = bell_draw(seeds[5], (N_SECTION, EXPERTS, D, H), D ** -0.5, 0.09375, ((0, 2), (1, 8), (2, 2)))
    down_weight = bell_draw(seeds[6], (N_SECTION, EXPERTS, H, D), H ** -0.5, 0.1875, ((0, 2), (1, 8), (3, 2)))
    routes = draw_routes(jax.random.fold_in(seeds[10], 71), 0)
    slots = draw_slots(jax.random.fold_in(seeds[10], 71), 0)
    affinity = jnp.clip(0.05 + 0.95 * jax.random.uniform(seeds[9], (4, N_SECTION, TOKENS, TOPK), jnp.float32) ** levels(seeds[9], (4, N_SECTION, TOKENS, TOPK), ((1, 2), (2, 16)), -0.2, 0.2), 0.05, 1.0)
    return dict(fwd_input=fwd_input, back_saved=back_saved, back_grad=back_grad, norm_gain=norm_gain, gate_weight=gate_weight, up_weight=up_weight, down_weight=down_weight, routes=routes, slots=slots, affinity=affinity)


ROUTE_SCALE = 2.5
EPSILON = 1e-06

def normalize(inputs, gain):
    widened = inputs.astype(jnp.float32)
    inverse = lax.rsqrt(lax.optimization_barrier(jnp.mean(widened * widened, axis=-1, keepdims=True)) + EPSILON)
    return (widened, inverse, (widened * inverse * gain).astype(jnp.bfloat16))

def contract_last(left, right):
    return lax.dot_general(left, right, (((1,), (1,)), ((), ())), preferred_element_type=jnp.float32)

def expert_forward(rows, gate_w, up_w, down_w):
    gate = jnp.dot(rows, gate_w, preferred_element_type=jnp.float32)
    upper = jnp.dot(rows, up_w, preferred_element_type=jnp.float32)
    active = (gate * jax.nn.sigmoid(gate) * upper).astype(jnp.bfloat16)
    return jnp.dot(active, down_w, preferred_element_type=jnp.float32).astype(jnp.bfloat16)

def swiglu_backward(gate, upper, dactive):
    sigma = jax.nn.sigmoid(gate)
    dgate = (dactive * upper * sigma * (1.0 + gate * (1.0 - sigma))).astype(jnp.bfloat16)
    dupper = (dactive * gate * sigma).astype(jnp.bfloat16)
    return (dgate, dupper)

def expert_backward(rows, grads, gate_w, up_w, down_w):
    gate = jnp.dot(rows, gate_w, preferred_element_type=jnp.float32)
    upper = jnp.dot(rows, up_w, preferred_element_type=jnp.float32)
    dactive = contract_last(grads, down_w)
    dgate, dupper = swiglu_backward(gate, upper, dactive)
    return (contract_last(dgate, gate_w) + contract_last(dupper, up_w)).astype(jnp.bfloat16)

def destinations(routes, slots):
    blocks = (jnp.arange(TOKENS) // TOK_DEV).astype(jnp.int32)
    return routes * (TOKENS // TOK_DEV * CAP) + blocks[:, None] * CAP + slots

def place_rows(values, targets):
    count = EXPERTS * (TOKENS // TOK_DEV) * CAP
    placed = jnp.zeros((count, D), jnp.bfloat16).at[targets.reshape(-1)].set(values.reshape(-1, D))
    return placed.reshape(EXPERTS, -1, D)

def layer_forward(inputs, gain, gate_w, up_w, down_w, routes, slots, affinity):
    widened, inverse, normed = normalize(inputs, gain)
    targets = destinations(routes, slots)
    placed = place_rows(jnp.broadcast_to(normed[:, None, :], (TOKENS, TOPK, D)), targets)
    outputs = lax.map(lambda parts: expert_forward(parts[0], parts[1], parts[2], parts[3]), (placed, gate_w, up_w, down_w))
    picked = outputs.reshape(-1, D)[targets].astype(jnp.float32)
    mixing = affinity / lax.optimization_barrier(jnp.sum(affinity, axis=-1, keepdims=True))
    return (widened + ROUTE_SCALE * lax.optimization_barrier(jnp.sum(mixing[:, :, None] * picked, axis=1))).astype(jnp.bfloat16)

def layer_backward(inputs, grads, gain, gate_w, up_w, down_w, routes, slots, affinity):
    widened, inverse, normed = normalize(inputs, gain)
    targets = destinations(routes, slots)
    mixing = affinity / lax.optimization_barrier(jnp.sum(affinity, axis=-1, keepdims=True))
    wide_grads = grads.astype(jnp.float32)
    sent = (ROUTE_SCALE * mixing[:, :, None] * wide_grads[:, None, :]).astype(jnp.bfloat16)
    placed = place_rows(jnp.broadcast_to(normed[:, None, :], (TOKENS, TOPK, D)), targets)
    placed_grads = place_rows(sent, targets)
    results = lax.map(lambda parts: expert_backward(parts[0], parts[1], parts[2], parts[3], parts[4]), (placed, placed_grads, gate_w, up_w, down_w))
    dnormed = lax.optimization_barrier(jnp.sum(results.reshape(-1, D)[targets].astype(jnp.float32), axis=1))
    weighted = dnormed * gain
    project = lax.optimization_barrier(jnp.mean(weighted * widened, axis=-1, keepdims=True))
    return (wide_grads + inverse * (weighted - widened * inverse * inverse * project)).astype(jnp.bfloat16)

def reference(fwd_input, back_saved, back_grad, norm_gain, gate_weight, up_weight, down_weight, routes, slots, affinity):

    def forward_section(section, inputs, index):
        return layer_forward(inputs, norm_gain[section], gate_weight[section], up_weight[section], down_weight[section], routes[index, section], slots[index, section], affinity[index, section])

    def backward_section(section, inputs, grads, index):
        return layer_backward(inputs, grads, norm_gain[section], gate_weight[section], up_weight[section], down_weight[section], routes[index, section], slots[index, section], affinity[index, section])
    blank = jnp.zeros((TOKENS, D), jnp.bfloat16)
    first = [forward_section(section, fwd_input[section], 0) for section in range(N_SECTION)]
    back_first = [backward_section(section, back_saved[0, section], back_grad[section], 1) for section in range(N_SECTION)]
    moved = [blank] + first[:-1]
    moved_back = back_first[1:] + [blank]
    final = [forward_section(section, moved[section], 2) for section in range(N_SECTION)]
    final_back = [backward_section(section, back_saved[1, section], moved_back[section], 3) for section in range(N_SECTION)]
    return (jnp.stack(final), jnp.stack(final_back))
```

```python
import jax
import jax.numpy as jnp
from jax import lax
from jax.sharding import PartitionSpec as P

ROUTE_SCALE = 2.5
EPSILON = 1e-06
F32 = jnp.float32
BF16 = jnp.bfloat16


def shift(block, axis, distance):
    devices = range(lax.axis_size(axis))
    route = [(i - distance, i) for i in devices if i - distance in devices]
    return lax.ppermute(block, axis, route)


def shift_across(block, distance):
    sections = range(lax.axis_size("section"))
    route = [
        (2 * (i - distance) + 1 - y, 2 * i + y)
        for i in sections
        if i - distance in sections
        for y in range(2)
    ]
    return lax.ppermute(block, ("section", "dp"), route)


def swap(block):
    return lax.ppermute(block, "dp", [(0, 1), (1, 0)])


def contract_last(left, right):
    return lax.dot_general(left, right, (((1,), (1,)), ((), ())), preferred_element_type=F32)


def dot(left, right):
    return jnp.dot(left, right, preferred_element_type=F32)


def body(
    fwd_input,
    back_saved,
    back_grad,
    norm_gain,
    gate_weight,
    up_weight,
    down_weight,
    routes,
    slots,
    affinity,
):
    experts = lax.axis_size("expert")
    me = lax.axis_index("dp")
    tokens, width = fwd_input.shape[1:]
    half = width // 2
    topk = routes.shape[3]
    capacity = tokens * topk // experts + 1
    rows = experts * capacity
    gate_w, up_w, down_w = gate_weight[0, 0], up_weight[0, 0], down_weight[0, 0]
    hidden = gate_w.shape[1]

    def columns(block, index):
        return lax.dynamic_slice_in_dim(block, index * half, half, axis=-1)

    gain = columns(norm_gain[0], me)

    def both(block):
        return jnp.concatenate([columns(block, me), swap(columns(block, 1 - me))])

    def inverse_of(block):
        wide = block.astype(F32)
        return lax.rsqrt(jnp.mean(wide * wide, axis=-1) + EPSILON)

    x_first, saved_first, saved_second = fwd_input[0], back_saved[0, 0], back_saved[1, 0]
    own_mixing = affinity[:, 0] / jnp.sum(affinity[:, 0], axis=-1, keepdims=True)
    own_target = routes[:, 0] * capacity + slots[:, 0]
    own_inverse = jnp.stack([inverse_of(b) for b in (x_first, saved_first, saved_second)])
    count = own_target.size
    small = jnp.concatenate(
        [own_target.astype(F32).reshape(-1), own_mixing.reshape(-1), own_inverse.reshape(-1)]
    )
    other = swap(small)
    other_target = other[:count].reshape(own_target.shape).astype(jnp.int32)
    target = jnp.concatenate([own_target, other_target + rows], axis=1)
    mixing = jnp.concatenate(
        [own_mixing, other[count : 2 * count].reshape(own_mixing.shape)], axis=1
    )
    inverse = jnp.concatenate([own_inverse, other[2 * count :].reshape(own_inverse.shape)], axis=1)

    cells = jnp.arange(2 * rows, dtype=jnp.int32)
    chosen = target[:, :, :, None] == cells
    pick = chosen.astype(BF16)
    pick_any = jnp.any(chosen, axis=2).astype(BF16)
    scale_of = jnp.sum(
        jnp.where(chosen, ROUTE_SCALE * mixing[:, :, :, None], 0.0), axis=(1, 2)
    )

    def place(values, index):
        return lax.dot_general(
            pick_any[index], values, (((0,), (0,)), ((), ())), preferred_element_type=F32
        )

    def across(values):
        block = values.astype(BF16).reshape(2, experts, capacity, half)
        block = lax.all_to_all(block, "expert", split_axis=1, concat_axis=1, tiled=True)
        return block.reshape(2 * rows, half)

    def normed(wide, inv):
        return (wide * inv[:, None] * gain).astype(BF16)

    def reduced(parts):
        mine = jnp.concatenate([p[:rows] for p in parts], axis=1)
        theirs = jnp.concatenate([p[rows:].astype(BF16) for p in parts], axis=1)
        total = mine + swap(theirs).astype(F32)
        return [total[:, i * hidden : (i + 1) * hidden] for i in range(len(parts))]

    def shared(block):
        return jnp.concatenate([block, swap(block)])

    def forward(x, inv, index):
        wide = x.astype(F32)
        arrived = across(place(normed(wide, inv), index))
        gate, upper = reduced([dot(arrived, gate_w), dot(arrived, up_w)])
        active = shared((gate * jax.nn.sigmoid(gate) * upper).astype(BF16))
        returned = across(dot(active, down_w))
        mix = ROUTE_SCALE * sum(
            mixing[index, :, k, None] * dot(pick[index, :, k], returned) for k in range(topk)
        )
        return (wide + mix).astype(BF16)

    def saved_part(x, inv, index):
        arrived = across(place(normed(x.astype(F32), inv), index))
        return reduced([dot(arrived, gate_w), dot(arrived, up_w)])

    def backward(x, inv, gate_upper, g, index):
        wide, wide_g = x.astype(F32), g.astype(F32)
        inv = inv[:, None]
        arrived = across(place(g, index) * scale_of[index][:, None])
        (dactive,) = reduced([contract_last(arrived, down_w)])
        gate, upper = gate_upper
        sigma = jax.nn.sigmoid(gate)
        dgate = (dactive * upper * sigma * (1.0 + gate * (1.0 - sigma))).astype(BF16)
        dupper = (dactive * gate * sigma).astype(BF16)
        both_d = shared(jnp.concatenate([dgate, dupper], axis=1))
        returned = across(
            contract_last(both_d[:, :hidden], gate_w) + contract_last(both_d[:, hidden:], up_w)
        )
        weighted = dot(pick_any[index], returned) * gain
        part = jnp.sum(weighted * wide, axis=-1)
        project = (part + jnp.roll(swap(part), tokens))[:, None] / width
        return (wide_g + inv * (weighted - wide * inv * inv * project)).astype(BF16)

    x0 = both(x_first)
    s0 = both(saved_first)
    g0 = both(back_grad[0])
    s1 = both(saved_second)

    first_out = forward(x0, inverse[0], 0)
    first_wide = first_out.astype(F32)
    squares = jnp.sum(first_wide * first_wide, axis=-1)
    x1 = shift(first_out, "section", 1)
    total = shift(squares, "section", 1) + jnp.roll(shift_across(squares, 1), tokens)
    first_back = backward(s0, inverse[1], saved_part(s0, inverse[1], 1), g0, 1)
    g1 = shift(first_back, "section", -1)
    final_out = forward(x1, lax.rsqrt(total / width + EPSILON), 2)
    final_back = backward(s1, inverse[2], saved_part(s1, inverse[2], 3), g1, 3)

    def whole(block):
        mine, theirs = block[:tokens], swap(block[tokens:])
        left = jnp.where(me == 0, mine, theirs)
        right = jnp.where(me == 0, theirs, mine)
        return jnp.concatenate([left, right], axis=1)[None]

    return (whole(final_out), whole(final_back))


def solution(mesh):
    placed = (
        P("section", ("expert", "dp"), None),
        P(None, "section", ("expert", "dp"), None),
        P("section", ("expert", "dp"), None),
        P("section", None),
        P("section", "expert", "dp", None),
        P("section", "expert", "dp", None),
        P("section", "expert", None, "dp"),
        P(None, "section", ("expert", "dp"), None),
        P(None, "section", ("expert", "dp"), None),
        P(None, "section", ("expert", "dp"), None),
    )
    return jax.shard_map(
        body,
        mesh=mesh,
        in_specs=placed,
        out_specs=(P("section", ("expert", "dp"), None), P("section", ("expert", "dp"), None)),
        check_vma=False,
    )
```

```python
import functools

import jax
import jax.numpy as jnp
from jax import lax
from jax.experimental import pallas as pl
from jax.experimental.pallas import tpu as pltpu
from jax.sharding import PartitionSpec as P

ROUTE_SCALE = 2.5
EPSILON = 1e-06
F32 = jnp.float32
BF16 = jnp.bfloat16
MESH = pl.DeviceIdType.MESH
TILE = 256


def swap(block):
    return lax.ppermute(block, "dp", [(0, 1), (1, 0)])


def contract_last(left, right):
    return lax.dot_general(left, right, (((1,), (1,)), ((), ())), preferred_element_type=F32)


def dot(left, right):
    return jnp.dot(left, right, preferred_element_type=F32)


def kernel(
    experts,
    sections,
    padded,
    x0_ref,
    s0_ref,
    g0_ref,
    s1_ref,
    inv_ref,
    gain_ref,
    pick_ref,
    place_ref,
    scale_ref,
    mix_ref,
    gate_ref,
    up_ref,
    down_ref,
    out_f_ref,
    out_b_ref,
    zs,
    zr,
    wide_s,
    wide_r,
    thin_s,
    thin_r,
    small_s,
    small_r,
    shift_s,
    shift_r,
    own,
    dgu,
    act,
    weighted_ref,
    z_send,
    z_recv,
    y_send,
    y_recv,
):
    section = lax.axis_index("section")
    me = lax.axis_index("expert")
    dp = lax.axis_index("dp")
    rows = experts * padded // 2
    total = experts * padded
    tokens2, half = x0_ref.shape
    tokens = tokens2 // 2
    hidden = gate_ref.shape[1]
    has_next = section < sections - 1
    has_prev = section > 0

    barrier = pltpu.get_barrier_semaphore()

    def greet(step, carry):
        pl.semaphore_signal(
            barrier, inc=1, device_id={"expert": lax.rem(me + step, experts)}, device_id_type=MESH
        )
        return carry

    lax.fori_loop(1, experts, greet, 0)
    pl.semaphore_signal(barrier, inc=1, device_id={"dp": 1 - dp}, device_id_type=MESH)

    @pl.when(has_next)
    def _():
        pl.semaphore_signal(barrier, inc=1, device_id={"section": section + 1}, device_id_type=MESH)

    @pl.when(has_prev)
    def _():
        pl.semaphore_signal(barrier, inc=1, device_id={"section": section - 1}, device_id_type=MESH)

    sides = jnp.minimum(section, 1) + jnp.minimum(sections - 1 - section, 1)
    pl.semaphore_wait(barrier, experts + sides)

    def tiles(extent, step):
        def run(j, carry):
            step(pl.ds(pl.multiple_of(j * TILE, TILE), TILE))
            return carry

        lax.fori_loop(0, extent // TILE, run, 0)

    def z_copy(a, step):
        target = lax.rem(me + step, experts)
        return pltpu.make_async_remote_copy(
            src_ref=zs.at[a, target],
            dst_ref=zr.at[a, me],
            send_sem=z_send.at[a, step],
            recv_sem=z_recv.at[a, step],
            device_id={"expert": target},
            device_id_type=MESH,
        )

    def z_start(a):
        def run(step, carry):
            z_copy(a, step).start()
            return carry

        lax.fori_loop(1, experts, run, 0)
        zr[a, pl.ds(me, 1)] = zs[a, pl.ds(me, 1)]

    def z_wait(a):
        def run(step, carry):
            z_copy(a, step).wait_recv()
            return carry

        lax.fori_loop(1, experts, run, 0)

    def z_drain(a):
        def run(step, carry):
            z_copy(a, step).wait_send()
            return carry

        lax.fori_loop(1, experts, run, 0)

    def swap_copy(src, dst, index):
        return pltpu.make_async_remote_copy(
            src_ref=src,
            dst_ref=dst,
            send_sem=y_send.at[index],
            recv_sem=y_recv.at[index],
            device_id={"dp": 1 - dp},
            device_id_type=MESH,
        )

    def wide_copy(k):
        return swap_copy(wide_s.at[k], wide_r.at[k], k)

    def thin_copy(k):
        return swap_copy(thin_s.at[k], thin_r.at[k], 6 + k)

    def small_copy(k):
        return swap_copy(small_s.at[k], small_r.at[k], 10 + k)

    def shift_copy(k, distance):
        return pltpu.make_async_remote_copy(
            src_ref=shift_s.at[k],
            dst_ref=shift_r.at[k],
            send_sem=y_send.at[13 + k],
            recv_sem=y_recv.at[13 + k],
            device_id={"section": section + distance},
            device_id_type=MESH,
        )

    def put(a, cols, values):
        zs[a, :, :, cols] = values.astype(BF16).reshape(experts, padded, TILE)

    def arrived(a):
        return zr[a].reshape(total, half)

    def arrived_cols(a, cols):
        return zr[a, :, :, cols].reshape(total, TILE)

    def split(part):
        parts = part.reshape(experts, 2, padded // 2, TILE)
        return parts[:, 0].reshape(rows, TILE), parts[:, 1].reshape(rows, TILE)

    def merge(mine, theirs):
        shape = (experts, 1, padded // 2, TILE)
        pair = [mine.astype(F32).reshape(shape), theirs.astype(F32).reshape(shape)]
        return jnp.concatenate(pair, axis=1).reshape(total, TILE).astype(BF16)

    def send_normed(x_ref, inverse, m, a):
        def step(cols):
            normed = (x_ref[:, cols].astype(F32) * inverse * gain_ref[:, cols]).astype(BF16)
            put(a, cols, dot(place_ref[m], normed))

        tiles(half, step)
        z_start(a)

    def send_grads(g_ref, m, a):
        def step(cols):
            put(a, cols, dot(place_ref[m], g_ref[:, cols]) * scale_ref[m])

        tiles(half, step)
        z_start(a)

    def gate_up(a, k):
        def step(cols):
            held = arrived(a)
            for n, w_ref in enumerate((gate_ref, up_ref)):
                mine, theirs = split(dot(held, w_ref[:, cols]))
                own[k, n, :, cols] = mine
                wide_s[k, n, :, cols] = theirs.astype(BF16)

        tiles(hidden, step)
        wide_copy(k).start()

    def active(k, t):
        wide_copy(k).wait_recv()

        def step(cols):
            gate = own[k, 0, :, cols] + wide_r[k, 0, :, cols].astype(F32)
            upper = own[k, 1, :, cols] + wide_r[k, 1, :, cols].astype(F32)
            thin_s[t, :, cols] = (gate * jax.nn.sigmoid(gate) * upper).astype(BF16)

        tiles(hidden, step)
        thin_copy(t).start()

    def down(t, a):
        thin_copy(t).wait_recv()

        def join(cols):
            act[:, cols] = merge(thin_s[t, :, cols], thin_r[t, :, cols])

        tiles(hidden, join)

        def step(cols):
            put(a, cols, dot(act[...], down_ref[:, cols]))

        tiles(half, step)
        z_start(a)

    def combine(x_ref, m, a, out_ref):
        def step(cols):
            returned = arrived_cols(a, cols)
            mixed = mix_ref[m, 0] * dot(pick_ref[m, 0], returned)
            mixed += mix_ref[m, 1] * dot(pick_ref[m, 1], returned)
            out_ref[:, cols] = (x_ref[:, cols].astype(F32) + ROUTE_SCALE * mixed).astype(BF16)

        tiles(half, step)

    def dactive(a, t):
        def step(cols):
            mine, theirs = split(contract_last(arrived(a), down_ref[cols, :]))
            own[4, 0, :, cols] = mine
            thin_s[t, :, cols] = theirs.astype(BF16)

        tiles(hidden, step)
        thin_copy(t).start()

    def dgate_up(k, t, w):
        wide_copy(k).wait_recv()
        thin_copy(t).wait_recv()

        def step(cols):
            gate = own[k, 0, :, cols] + wide_r[k, 0, :, cols].astype(F32)
            upper = own[k, 1, :, cols] + wide_r[k, 1, :, cols].astype(F32)
            dact = own[4, 0, :, cols] + thin_r[t, :, cols].astype(F32)
            sigma = jax.nn.sigmoid(gate)
            dgate = dact * upper * sigma * (1.0 + gate * (1.0 - sigma))
            wide_s[w, 0, :, cols] = dgate.astype(BF16)
            wide_s[w, 1, :, cols] = (dact * gate * sigma).astype(BF16)

        tiles(hidden, step)
        wide_copy(w).start()

    def dexpert(w, a):
        wide_copy(w).wait_recv()

        def join(cols):
            for n in range(2):
                dgu[n, :, cols] = merge(wide_s[w, n, :, cols], wide_r[w, n, :, cols])

        tiles(hidden, join)

        def step(cols):
            put(
                a,
                cols,
                contract_last(dgu[0], gate_ref[cols, :]) + contract_last(dgu[1], up_ref[cols, :]),
            )

        tiles(half, step)
        z_start(a)

    def summed(part, k):
        small_s[k] = jnp.broadcast_to(part, (tokens2, 128))
        small_copy(k).start()
        small_copy(k).wait_recv()
        theirs = small_r[k]
        both = jnp.concatenate([theirs[tokens:], theirs[:tokens]])
        return (part + both[:, :1]) / width

    width = 2 * half

    def gradient(x_ref, inverse, g_ref, m, a, k, out_ref):
        def first(j, part):
            cols = pl.ds(pl.multiple_of(j * TILE, TILE), TILE)
            returned = arrived_cols(a, cols)
            dnormed = dot(pick_ref[m, 0], returned) + dot(pick_ref[m, 1], returned)
            weighted = dnormed * gain_ref[:, cols]
            weighted_ref[:, cols] = weighted
            return part + jnp.sum(weighted * x_ref[:, cols].astype(F32), axis=-1, keepdims=True)

        part = lax.fori_loop(0, half // TILE, first, jnp.zeros((tokens2, 1), F32))
        project = summed(part, k)

        def step(cols):
            wide = x_ref[:, cols].astype(F32)
            change = inverse * (weighted_ref[:, cols] - wide * inverse * inverse * project)
            out_ref[:, cols] = (g_ref[:, cols].astype(F32) + change).astype(BF16)

        tiles(half, step)

    x1_ref, g1_ref = shift_r.at[0], shift_r.at[1]

    @pl.when(section == 0)
    def _():
        shift_r[0] = jnp.zeros((tokens2, half), BF16)

    @pl.when(section == sections - 1)
    def _():
        shift_r[1] = jnp.zeros((tokens2, half), BF16)

    send_normed(x0_ref, inv_ref[0], 0, 0)
    send_normed(s0_ref, inv_ref[1], 1, 1)
    send_grads(g0_ref, 1, 2)
    z_wait(0)
    gate_up(0, 0)
    z_wait(1)
    gate_up(1, 1)
    active(0, 0)
    down(0, 4)
    send_normed(s1_ref, inv_ref[2], 3, 3)
    z_wait(2)
    dactive(2, 1)
    dgate_up(1, 1, 4)
    dexpert(4, 5)
    z_wait(4)
    combine(x0_ref, 0, 4, shift_s.at[0])

    @pl.when(has_next)
    def _():
        shift_copy(0, 1).start()

    z_wait(3)
    gate_up(3, 3)

    @pl.when(has_prev)
    def _():
        shift_copy(0, 1).wait_recv()

    def squares(j, part):
        wide = x1_ref[:, pl.ds(pl.multiple_of(j * TILE, TILE), TILE)].astype(F32)
        return part + jnp.sum(wide * wide, axis=-1, keepdims=True)

    part = lax.fori_loop(0, half // TILE, squares, jnp.zeros((tokens2, 1), F32))
    send_normed(x1_ref, lax.rsqrt(summed(part, 0) + EPSILON), 2, 6)
    z_wait(5)
    gradient(s0_ref, inv_ref[1], g0_ref, 1, 5, 1, shift_s.at[1])

    @pl.when(has_prev)
    def _():
        shift_copy(1, -1).start()

    @pl.when(has_next)
    def _():
        shift_copy(1, -1).wait_recv()

    send_grads(g1_ref, 3, 7)
    z_wait(6)
    gate_up(6, 2)
    active(2, 2)
    down(2, 8)
    z_wait(7)
    dactive(7, 3)
    dgate_up(3, 3, 5)
    dexpert(5, 9)
    z_wait(8)
    combine(x1_ref, 2, 8, out_f_ref)
    z_wait(9)
    gradient(s1_ref, inv_ref[2], g1_ref, 3, 9, 2, out_b_ref)

    for a in range(10):
        z_drain(a)
    for k in range(6):
        wide_copy(k).wait_send()
    for k in range(4):
        thin_copy(k).wait_send()
    for k in range(3):
        small_copy(k).wait_send()

    @pl.when(has_next)
    def _():
        shift_copy(0, 1).wait_send()

    @pl.when(has_prev)
    def _():
        shift_copy(1, -1).wait_send()


def body(
    fwd_input,
    back_saved,
    back_grad,
    norm_gain,
    gate_weight,
    up_weight,
    down_weight,
    routes,
    slots,
    affinity,
):
    experts = lax.axis_size("expert")
    me = lax.axis_index("dp")
    tokens, width = fwd_input.shape[1:]
    half = width // 2
    topk = routes.shape[3]
    capacity = tokens * topk // experts + 1
    padded = -(-capacity // 8) * 16
    rows = experts * padded // 2
    gate_w, up_w, down_w = gate_weight[0, 0], up_weight[0, 0], down_weight[0, 0]
    hidden = gate_w.shape[1]

    def columns(block, index):
        return lax.dynamic_slice_in_dim(block, index * half, half, axis=-1)

    gain = columns(norm_gain[0], me)

    def both(block):
        return jnp.concatenate([columns(block, me), swap(columns(block, 1 - me))])

    def inverse_of(block):
        wide = block.astype(F32)
        return lax.rsqrt(jnp.mean(wide * wide, axis=-1) + EPSILON)

    x_first, saved_first, saved_second = fwd_input[0], back_saved[0, 0], back_saved[1, 0]
    own_mixing = affinity[:, 0] / jnp.sum(affinity[:, 0], axis=-1, keepdims=True)
    own_target = routes[:, 0] * padded + slots[:, 0]
    own_inverse = jnp.stack([inverse_of(b) for b in (x_first, saved_first, saved_second)])
    count = own_target.size
    small = jnp.concatenate(
        [own_target.astype(F32).reshape(-1), own_mixing.reshape(-1), own_inverse.reshape(-1)]
    )
    other = swap(small)
    other_target = other[:count].reshape(own_target.shape).astype(jnp.int32)
    target = jnp.concatenate([own_target, other_target + padded // 2], axis=1)
    mixing = jnp.concatenate(
        [own_mixing, other[count : 2 * count].reshape(own_mixing.shape)], axis=1
    )
    inverse = jnp.concatenate([own_inverse, other[2 * count :].reshape(own_inverse.shape)], axis=1)

    cells = jnp.arange(2 * rows, dtype=jnp.int32)
    chosen = target[:, :, :, None] == cells
    pick = jnp.swapaxes(chosen, 1, 2).astype(BF16)
    place = (
        (target[:, None, :, 0] == cells[:, None]) | (target[:, None, :, 1] == cells[:, None])
    ).astype(BF16)
    scale = jnp.sum(
        jnp.where(chosen, ROUTE_SCALE * mixing[:, :, :, None], 0.0), axis=(1, 2)
    )[:, :, None]
    mix = jnp.swapaxes(mixing, 1, 2)[:, :, :, None]
    token_pairs = 2 * tokens
    vmem = pl.BlockSpec(memory_space=pltpu.VMEM)
    sections = lax.axis_size("section")
    operands = (
        both(x_first),
        both(saved_first),
        both(back_grad[0]),
        both(saved_second),
        inverse[:, :, None],
        gain[None],
        pick,
        place,
        scale,
        mix,
        gate_w,
        up_w,
        down_w,
    )
    final_out, final_back = pl.pallas_call(
        functools.partial(kernel, experts, sections, padded),
        out_shape=[jax.ShapeDtypeStruct((token_pairs, half), BF16)] * 2,
        in_specs=[vmem] * len(operands),
        out_specs=[vmem] * 2,
        scratch_shapes=[
            pltpu.VMEM((10, experts, padded, half), BF16),
            pltpu.VMEM((10, experts, padded, half), BF16),
            pltpu.VMEM((6, 2, rows, hidden), BF16),
            pltpu.VMEM((6, 2, rows, hidden), BF16),
            pltpu.VMEM((4, rows, hidden), BF16),
            pltpu.VMEM((4, rows, hidden), BF16),
            pltpu.VMEM((3, token_pairs, 128), F32),
            pltpu.VMEM((3, token_pairs, 128), F32),
            pltpu.VMEM((2, token_pairs, half), BF16),
            pltpu.VMEM((2, token_pairs, half), BF16),
            pltpu.VMEM((5, 2, rows, hidden), F32),
            pltpu.VMEM((2, 2 * rows, hidden), BF16),
            pltpu.VMEM((2 * rows, hidden), BF16),
            pltpu.VMEM((token_pairs, half), F32),
            pltpu.SemaphoreType.DMA((10, experts)),
            pltpu.SemaphoreType.DMA((10, experts)),
            pltpu.SemaphoreType.DMA((15,)),
            pltpu.SemaphoreType.DMA((15,)),
        ],
        compiler_params=pltpu.CompilerParams(
            collective_id=0, has_side_effects=True, vmem_limit_bytes=62 * 1024 * 1024
        ),
    )(*operands)

    def whole(block):
        mine, theirs = block[:tokens], swap(block[tokens:])
        left = jnp.where(me == 0, mine, theirs)
        right = jnp.where(me == 0, theirs, mine)
        return jnp.concatenate([left, right], axis=1)[None]

    return (whole(final_out), whole(final_back))


def solution(mesh):
    placed = (
        P("section", ("expert", "dp"), None),
        P(None, "section", ("expert", "dp"), None),
        P("section", ("expert", "dp"), None),
        P("section", None),
        P("section", "expert", "dp", None),
        P("section", "expert", "dp", None),
        P("section", "expert", None, "dp"),
        P(None, "section", ("expert", "dp"), None),
        P(None, "section", ("expert", "dp"), None),
        P(None, "section", ("expert", "dp"), None),
    )
    return jax.shard_map(
        body,
        mesh=mesh,
        in_specs=placed,
        out_specs=(P("section", ("expert", "dp"), None), P("section", ("expert", "dp"), None)),
        check_vma=False,
    )
```

```python
import functools

import jax
import jax.numpy as jnp
from jax import lax
from jax.experimental import pallas as pl
from jax.experimental.pallas import tpu as pltpu
from jax.sharding import PartitionSpec as P

ROUTE_SCALE = 2.5
EPSILON = 1e-06
F32 = jnp.float32
BF16 = jnp.bfloat16
MESH = pl.DeviceIdType.MESH
TILE = 256


def swap(block):
    return lax.ppermute(block, "dp", [(0, 1), (1, 0)])


def contract_last(left, right):
    return lax.dot_general(left, right, (((1,), (1,)), ((), ())), preferred_element_type=F32)


def dot(left, right):
    return jnp.dot(left, right, preferred_element_type=F32)


def kernel(
    experts,
    sections,
    padded,
    x0_ref,
    s0_ref,
    g0_ref,
    s1_ref,
    inv_ref,
    gain_ref,
    pick_ref,
    place_ref,
    scale_ref,
    mix_ref,
    gate_ref,
    up_ref,
    down_ref,
    out_f_ref,
    out_b_ref,
    zs,
    zr,
    wide_s,
    wide_r,
    thin_s,
    thin_r,
    small_s,
    small_r,
    shift_s,
    shift_r,
    own,
    dgu,
    act,
    weighted_ref,
    fin,
    fin_r,
    z_send,
    z_recv,
    y_send,
    y_recv,
):
    section = lax.axis_index("section")
    me = lax.axis_index("expert")
    dp = lax.axis_index("dp")
    rows = experts * padded // 2
    total = experts * padded
    tokens2, half = x0_ref.shape
    tokens = tokens2 // 2
    hidden = gate_ref.shape[1]
    has_next = section < sections - 1
    has_prev = section > 0

    barrier = pltpu.get_barrier_semaphore()

    def greet(step, carry):
        pl.semaphore_signal(
            barrier, inc=1, device_id={"expert": lax.rem(me + step, experts)}, device_id_type=MESH
        )
        return carry

    lax.fori_loop(1, experts, greet, 0)
    pl.semaphore_signal(barrier, inc=1, device_id={"dp": 1 - dp}, device_id_type=MESH)

    @pl.when(has_next)
    def _():
        pl.semaphore_signal(barrier, inc=1, device_id={"section": section + 1}, device_id_type=MESH)

    @pl.when(has_prev)
    def _():
        pl.semaphore_signal(barrier, inc=1, device_id={"section": section - 1}, device_id_type=MESH)

    sides = jnp.minimum(section, 1) + jnp.minimum(sections - 1 - section, 1)
    pl.semaphore_wait(barrier, experts + sides)

    def tiles(extent, step):
        def run(j, carry):
            step(pl.ds(pl.multiple_of(j * TILE, TILE), TILE))
            return carry

        lax.fori_loop(0, extent // TILE, run, 0)

    def z_copy(a, step):
        target = lax.rem(me + step, experts)
        return pltpu.make_async_remote_copy(
            src_ref=zs.at[a, target],
            dst_ref=zr.at[a, me],
            send_sem=z_send.at[a, step],
            recv_sem=z_recv.at[a, step],
            device_id={"expert": target},
            device_id_type=MESH,
        )

    def z_start(a):
        def run(step, carry):
            z_copy(a, step).start()
            return carry

        lax.fori_loop(1, experts, run, 0)
        zr[a, pl.ds(me, 1)] = zs[a, pl.ds(me, 1)]

    def z_wait(a):
        def run(step, carry):
            z_copy(a, step).wait_recv()
            return carry

        lax.fori_loop(1, experts, run, 0)

    def z_drain(a):
        def run(step, carry):
            z_copy(a, step).wait_send()
            return carry

        lax.fori_loop(1, experts, run, 0)

    def swap_copy(src, dst, index):
        return pltpu.make_async_remote_copy(
            src_ref=src,
            dst_ref=dst,
            send_sem=y_send.at[index],
            recv_sem=y_recv.at[index],
            device_id={"dp": 1 - dp},
            device_id_type=MESH,
        )

    def wide_copy(k):
        return swap_copy(wide_s.at[k], wide_r.at[k], k)

    def thin_copy(k):
        return swap_copy(thin_s.at[k], thin_r.at[k], 6 + k)

    def small_copy(k):
        return swap_copy(small_s.at[k], small_r.at[k], 10 + k)

    def shift_copy(k, distance):
        return pltpu.make_async_remote_copy(
            src_ref=shift_s.at[k],
            dst_ref=shift_r.at[k],
            send_sem=y_send.at[13 + k],
            recv_sem=y_recv.at[13 + k],
            device_id={"section": section + distance},
            device_id_type=MESH,
        )

    def put(a, cols, values):
        zs[a, :, :, cols] = values.astype(BF16).reshape(experts, padded, TILE)

    def arrived(a):
        return zr[a].reshape(total, half)

    def arrived_cols(a, cols):
        return zr[a, :, :, cols].reshape(total, TILE)

    def split(part):
        parts = part.reshape(experts, 2, padded // 2, TILE)
        return parts[:, 0].reshape(rows, TILE), parts[:, 1].reshape(rows, TILE)

    def merge(mine, theirs):
        shape = (experts, 1, padded // 2, TILE)
        pair = [mine.astype(F32).reshape(shape), theirs.astype(F32).reshape(shape)]
        return jnp.concatenate(pair, axis=1).reshape(total, TILE).astype(BF16)

    def send_normed(x_ref, inverse, m, a):
        def step(cols):
            normed = (x_ref[:, cols].astype(F32) * inverse * gain_ref[:, cols]).astype(BF16)
            put(a, cols, dot(place_ref[m], normed))

        tiles(half, step)
        z_start(a)

    def send_grads(g_ref, m, a):
        def step(cols):
            put(a, cols, dot(place_ref[m], g_ref[:, cols]) * scale_ref[m])

        tiles(half, step)
        z_start(a)

    def gate_up(a, k):
        def step(cols):
            held = arrived(a)
            for n, w_ref in enumerate((gate_ref, up_ref)):
                mine, theirs = split(dot(held, w_ref[:, cols]))
                own[k, n, :, cols] = mine
                wide_s[k, n, :, cols] = theirs.astype(BF16)

        tiles(hidden, step)
        wide_copy(k).start()

    def active(k, t):
        wide_copy(k).wait_recv()

        def step(cols):
            gate = own[k, 0, :, cols] + wide_r[k, 0, :, cols].astype(F32)
            upper = own[k, 1, :, cols] + wide_r[k, 1, :, cols].astype(F32)
            thin_s[t, :, cols] = (gate * jax.nn.sigmoid(gate) * upper).astype(BF16)

        tiles(hidden, step)
        thin_copy(t).start()

    def down(t, a):
        thin_copy(t).wait_recv()

        def join(cols):
            act[:, cols] = merge(thin_s[t, :, cols], thin_r[t, :, cols])

        tiles(hidden, join)

        def step(cols):
            put(a, cols, dot(act[...], down_ref[:, cols]))

        tiles(half, step)
        z_start(a)

    def combine(x_ref, m, a, out_ref):
        def step(cols):
            returned = arrived_cols(a, cols)
            mixed = mix_ref[m, 0] * dot(pick_ref[m, 0], returned)
            mixed += mix_ref[m, 1] * dot(pick_ref[m, 1], returned)
            out_ref[:, cols] = (x_ref[:, cols].astype(F32) + ROUTE_SCALE * mixed).astype(BF16)

        tiles(half, step)

    def dactive(a, t):
        def step(cols):
            mine, theirs = split(contract_last(arrived(a), down_ref[cols, :]))
            own[4, 0, :, cols] = mine
            thin_s[t, :, cols] = theirs.astype(BF16)

        tiles(hidden, step)
        thin_copy(t).start()

    def dgate_up(k, t, w):
        wide_copy(k).wait_recv()
        thin_copy(t).wait_recv()

        def step(cols):
            gate = own[k, 0, :, cols] + wide_r[k, 0, :, cols].astype(F32)
            upper = own[k, 1, :, cols] + wide_r[k, 1, :, cols].astype(F32)
            dact = own[4, 0, :, cols] + thin_r[t, :, cols].astype(F32)
            sigma = jax.nn.sigmoid(gate)
            dgate = dact * upper * sigma * (1.0 + gate * (1.0 - sigma))
            wide_s[w, 0, :, cols] = dgate.astype(BF16)
            wide_s[w, 1, :, cols] = (dact * gate * sigma).astype(BF16)

        tiles(hidden, step)
        wide_copy(w).start()

    def dexpert(w, a):
        wide_copy(w).wait_recv()

        def join(cols):
            for n in range(2):
                dgu[n, :, cols] = merge(wide_s[w, n, :, cols], wide_r[w, n, :, cols])

        tiles(hidden, join)

        def step(cols):
            put(
                a,
                cols,
                contract_last(dgu[0], gate_ref[cols, :]) + contract_last(dgu[1], up_ref[cols, :]),
            )

        tiles(half, step)
        z_start(a)

    def summed(part, k):
        small_s[k] = jnp.broadcast_to(part, (tokens2, 128))
        small_copy(k).start()
        small_copy(k).wait_recv()
        theirs = small_r[k]
        both = jnp.concatenate([theirs[tokens:], theirs[:tokens]])
        return (part + both[:, :1]) / width

    width = 2 * half

    def gradient(x_ref, inverse, g_ref, m, a, k, out_ref):
        def first(j, part):
            cols = pl.ds(pl.multiple_of(j * TILE, TILE), TILE)
            returned = arrived_cols(a, cols)
            dnormed = dot(pick_ref[m, 0], returned) + dot(pick_ref[m, 1], returned)
            weighted = dnormed * gain_ref[:, cols]
            weighted_ref[:, cols] = weighted
            return part + jnp.sum(weighted * x_ref[:, cols].astype(F32), axis=-1, keepdims=True)

        part = lax.fori_loop(0, half // TILE, first, jnp.zeros((tokens2, 1), F32))
        project = summed(part, k)

        def step(cols):
            wide = x_ref[:, cols].astype(F32)
            change = inverse * (weighted_ref[:, cols] - wide * inverse * inverse * project)
            out_ref[:, cols] = (g_ref[:, cols].astype(F32) + change).astype(BF16)

        tiles(half, step)

    def final_copy(k):
        return swap_copy(fin.at[k, pl.ds(tokens, tokens)], fin_r.at[k], 15 + k)

    def finish(k, out_ref):
        final_copy(k).wait_recv()

        def run(j, carry):
            cols = pl.ds(pl.multiple_of(j * TILE, TILE), TILE)
            mine = pl.ds(pl.multiple_of(dp * half + j * TILE, TILE), TILE)
            theirs = pl.ds(pl.multiple_of((1 - dp) * half + j * TILE, TILE), TILE)
            out_ref[:, mine] = fin[k, :tokens, cols]
            out_ref[:, theirs] = fin_r[k, :, cols]
            return carry

        lax.fori_loop(0, half // TILE, run, 0)

    x1_ref, g1_ref = shift_r.at[0], shift_r.at[1]

    @pl.when(section == 0)
    def _():
        shift_r[0] = jnp.zeros((tokens2, half), BF16)

    @pl.when(section == sections - 1)
    def _():
        shift_r[1] = jnp.zeros((tokens2, half), BF16)

    send_normed(x0_ref, inv_ref[0], 0, 0)
    send_normed(s0_ref, inv_ref[1], 1, 1)
    send_grads(g0_ref, 1, 2)
    z_wait(0)
    gate_up(0, 0)
    z_wait(1)
    gate_up(1, 1)
    active(0, 0)
    down(0, 4)
    send_normed(s1_ref, inv_ref[2], 3, 3)
    z_wait(2)
    dactive(2, 1)
    dgate_up(1, 1, 4)
    dexpert(4, 5)
    z_wait(4)
    combine(x0_ref, 0, 4, shift_s.at[0])

    @pl.when(has_next)
    def _():
        shift_copy(0, 1).start()

    z_wait(3)
    gate_up(3, 3)

    @pl.when(has_prev)
    def _():
        shift_copy(0, 1).wait_recv()

    def squares(j, part):
        wide = x1_ref[:, pl.ds(pl.multiple_of(j * TILE, TILE), TILE)].astype(F32)
        return part + jnp.sum(wide * wide, axis=-1, keepdims=True)

    part = lax.fori_loop(0, half // TILE, squares, jnp.zeros((tokens2, 1), F32))
    send_normed(x1_ref, lax.rsqrt(summed(part, 0) + EPSILON), 2, 6)
    z_wait(5)
    gradient(s0_ref, inv_ref[1], g0_ref, 1, 5, 1, shift_s.at[1])

    @pl.when(has_prev)
    def _():
        shift_copy(1, -1).start()

    @pl.when(has_next)
    def _():
        shift_copy(1, -1).wait_recv()

    send_grads(g1_ref, 3, 7)
    z_wait(6)
    gate_up(6, 2)
    active(2, 2)
    down(2, 8)
    z_wait(7)
    dactive(7, 3)
    dgate_up(3, 3, 5)
    dexpert(5, 9)
    z_wait(8)
    combine(x1_ref, 2, 8, fin.at[0])
    final_copy(0).start()
    z_wait(9)
    gradient(s1_ref, inv_ref[2], g1_ref, 3, 9, 2, fin.at[1])
    final_copy(1).start()
    finish(0, out_f_ref)
    finish(1, out_b_ref)

    for a in range(10):
        z_drain(a)
    for k in range(6):
        wide_copy(k).wait_send()
    for k in range(4):
        thin_copy(k).wait_send()
    for k in range(3):
        small_copy(k).wait_send()
    for k in range(2):
        final_copy(k).wait_send()

    @pl.when(has_next)
    def _():
        shift_copy(0, 1).wait_send()

    @pl.when(has_prev)
    def _():
        shift_copy(1, -1).wait_send()


def body(
    fwd_input,
    back_saved,
    back_grad,
    norm_gain,
    gate_weight,
    up_weight,
    down_weight,
    routes,
    slots,
    affinity,
):
    experts = lax.axis_size("expert")
    me = lax.axis_index("dp")
    tokens, width = fwd_input.shape[1:]
    half = width // 2
    topk = routes.shape[3]
    capacity = tokens * topk // experts + 1
    padded = -(-capacity // 8) * 16
    rows = experts * padded // 2
    gate_w, up_w, down_w = gate_weight[0, 0], up_weight[0, 0], down_weight[0, 0]
    hidden = gate_w.shape[1]

    def columns(block, index):
        return lax.dynamic_slice_in_dim(block, index * half, half, axis=-1)

    gain = columns(norm_gain[0], me)

    def both(block):
        return jnp.concatenate([columns(block, me), swap(columns(block, 1 - me))])

    def inverse_of(block):
        wide = block.astype(F32)
        return lax.rsqrt(jnp.mean(wide * wide, axis=-1) + EPSILON)

    x_first, saved_first, saved_second = fwd_input[0], back_saved[0, 0], back_saved[1, 0]
    own_mixing = affinity[:, 0] / jnp.sum(affinity[:, 0], axis=-1, keepdims=True)
    own_target = routes[:, 0] * padded + slots[:, 0]
    own_inverse = jnp.stack([inverse_of(b) for b in (x_first, saved_first, saved_second)])
    count = own_target.size
    small = jnp.concatenate(
        [own_target.astype(F32).reshape(-1), own_mixing.reshape(-1), own_inverse.reshape(-1)]
    )
    other = swap(small)
    other_target = other[:count].reshape(own_target.shape).astype(jnp.int32)
    target = jnp.concatenate([own_target, other_target + padded // 2], axis=1)
    mixing = jnp.concatenate(
        [own_mixing, other[count : 2 * count].reshape(own_mixing.shape)], axis=1
    )
    inverse = jnp.concatenate([own_inverse, other[2 * count :].reshape(own_inverse.shape)], axis=1)

    cells = jnp.arange(2 * rows, dtype=jnp.int32)
    chosen = target[:, :, :, None] == cells
    pick = jnp.swapaxes(chosen, 1, 2).astype(BF16)
    place = (
        (target[:, None, :, 0] == cells[:, None]) | (target[:, None, :, 1] == cells[:, None])
    ).astype(BF16)
    scale = jnp.sum(
        jnp.where(chosen, ROUTE_SCALE * mixing[:, :, :, None], 0.0), axis=(1, 2)
    )[:, :, None]
    mix = jnp.swapaxes(mixing, 1, 2)[:, :, :, None]
    token_pairs = 2 * tokens
    vmem = pl.BlockSpec(memory_space=pltpu.VMEM)
    sections = lax.axis_size("section")
    operands = (
        both(x_first),
        both(saved_first),
        both(back_grad[0]),
        both(saved_second),
        inverse[:, :, None],
        gain[None],
        pick,
        place,
        scale,
        mix,
        gate_w,
        up_w,
        down_w,
    )
    final_out, final_back = pl.pallas_call(
        functools.partial(kernel, experts, sections, padded),
        out_shape=[jax.ShapeDtypeStruct((tokens, width), BF16)] * 2,
        in_specs=[vmem] * len(operands),
        out_specs=[vmem] * 2,
        scratch_shapes=[
            pltpu.VMEM((10, experts, padded, half), BF16),
            pltpu.VMEM((10, experts, padded, half), BF16),
            pltpu.VMEM((6, 2, rows, hidden), BF16),
            pltpu.VMEM((6, 2, rows, hidden), BF16),
            pltpu.VMEM((4, rows, hidden), BF16),
            pltpu.VMEM((4, rows, hidden), BF16),
            pltpu.VMEM((3, token_pairs, 128), F32),
            pltpu.VMEM((3, token_pairs, 128), F32),
            pltpu.VMEM((2, token_pairs, half), BF16),
            pltpu.VMEM((2, token_pairs, half), BF16),
            pltpu.VMEM((5, 2, rows, hidden), F32),
            pltpu.VMEM((2, 2 * rows, hidden), BF16),
            pltpu.VMEM((2 * rows, hidden), BF16),
            pltpu.VMEM((token_pairs, half), F32),
            pltpu.VMEM((2, token_pairs, half), BF16),
            pltpu.VMEM((2, tokens, half), BF16),
            pltpu.SemaphoreType.DMA((10, experts)),
            pltpu.SemaphoreType.DMA((10, experts)),
            pltpu.SemaphoreType.DMA((17,)),
            pltpu.SemaphoreType.DMA((17,)),
        ],
        compiler_params=pltpu.CompilerParams(
            collective_id=0, has_side_effects=True, vmem_limit_bytes=62 * 1024 * 1024
        ),
    )(*operands)

    return (final_out[None], final_back[None])


def solution(mesh):
    placed = (
        P("section", ("expert", "dp"), None),
        P(None, "section", ("expert", "dp"), None),
        P("section", ("expert", "dp"), None),
        P("section", None),
        P("section", "expert", "dp", None),
        P("section", "expert", "dp", None),
        P("section", "expert", None, "dp"),
        P(None, "section", ("expert", "dp"), None),
        P(None, "section", ("expert", "dp"), None),
        P(None, "section", ("expert", "dp"), None),
    )
    return jax.shard_map(
        body,
        mesh=mesh,
        in_specs=placed,
        out_specs=(P("section", ("expert", "dp"), None), P("section", ("expert", "dp"), None)),
        check_vma=False,
    )
```
